32 devices in a mesh: section: 4 (over x, core), tm: 4 (over z), space: 2 (over y).
Axes of the slice: x: 2, y: 2, z: 4, core: 2. Of those that a mesh axis runs over, the one named last changes fastest.
Arguments:
- video: bfloat16 [4, 8, 128, 1152], P('section', 'tm', 'space'), may hold values from -6 to 6
- conv_taps: float32 [4, 3, 1152], P('section'), may hold values from -3 to 3
- modulation: float32 [4, 6, 1152], P('section'), may hold values from -3 to 3
- w_qkv: bfloat16 [4, 1152, 3, 1152], P('section', None, None, 'space'), may hold values from -6 to 6
- w_out: bfloat16 [4, 1152, 1152], P('section', 'space'), may hold values from -0.1875 to 0.1875
- w_up: bfloat16 [4, 1152, 4608], P('section', None, 'space'), may hold values from -0.1875 to 0.1875
- w_down: bfloat16 [4, 4608, 1152], P('section', 'space'), may hold values from -0.09375 to 0.09375
Outputs:
- next_in: bfloat16 [4, 8, 128, 1152], P('section', 'tm', 'space')
The draws below stay inside these ranges and needn't reach their ends.
All inputs are finite; a program needn't handle non-finite values.
Results may differ from the reference program's by a relative error of at most 0.013.
Values may be sent and summed in bfloat16 or wider, within the bound.
A program may use at most 64 MiB of HBM per device.

```python
import math
import jax
import jax.numpy as jnp
from jax import lax

D = 1152
HEADS = 16
FF = 4608
LAYERS = 4
FRAMES = 8
HW = 128
N_SPACE = 2


def draw_w_qkv(key, part):
    sampled = jax.random.truncated_normal(key, -5.0, 5.0, (LAYERS, D, 3, D), jnp.float32) / jnp.sqrt(jnp.float32(D))
    return sampled.astype(jnp.bfloat16)


def level_of(key, extent, shards, low, high):
    level, own = 1.0, jax.random.fold_in(key, 6)
    for position, parts in shards:
        heights = jnp.exp(jax.random.uniform(jax.random.fold_in(own, position), (parts,), jnp.float32, low / len(shards), high / len(shards)))
        level = level * jnp.repeat(heights, extent[position] // parts).reshape([-1 if axis == position else 1 for axis in range(len(extent))])
    return level


def scatter_about(rng, shape, spread, most, cuts=(), dtype=jnp.bfloat16):
    gain = level_of(rng, shape, cuts, -0.22, 0.18) if cuts else 1.0
    drawn = jax.random.normal(rng, shape, jnp.float32) * spread * gain
    return jnp.minimum(jnp.maximum(drawn, -most), most).astype(dtype)


def setup_inputs(seed: int = 0) -> dict:
    splits = jax.random.split(jax.random.key(seed), 8)
    video = scatter_about(splits[0], (LAYERS, FRAMES, HW, D), 1.0, 6.0, ((0, 4), (1, 4), (2, 2)))
    conv_taps = scatter_about(splits[1], (LAYERS, 3, D), 0.5, 3.0, ((0, 4),), jnp.float32)
    modulation = scatter_about(splits[2], (LAYERS, 6, D), 0.5, 3.0, ((0, 4),), jnp.float32)
    w_qkv = draw_w_qkv(jax.random.fold_in(splits[7], 71), 0)
    w_out = scatter_about(splits[4], (LAYERS, D, D), D ** -0.5, 0.1875, ((0, 4), (1, 2)))
    w_up = scatter_about(splits[5], (LAYERS, D, FF), D ** -0.5, 0.1875, ((0, 4), (2, 2)))
    w_down = scatter_about(splits[6], (LAYERS, FF, D), FF ** -0.5, 0.09375, ((0, 4), (1, 2)))
    return dict(video=video, conv_taps=conv_taps, modulation=modulation, w_qkv=w_qkv, w_out=w_out, w_up=w_up, w_down=w_down)


def normalize(values_in):
    centre = lax.optimization_barrier(jnp.mean(values_in, axis=-1, keepdims=True))
    variance = lax.optimization_barrier(jnp.mean(jnp.square(values_in - centre), axis=-1, keepdims=True))
    return (values_in - centre) * lax.rsqrt(variance + 1e-06)

def modulated(values_in, shift_row, scale_row):
    return (normalize(values_in) * (1.0 + scale_row) + shift_row).astype(jnp.bfloat16)

def one_layer(slices):
    frames_in, tap_set, mod_table, query_w, out_w, up_w, down_w = slices
    frames_f32 = frames_in.astype(jnp.float32)
    padded = jnp.concatenate([jnp.zeros((2,) + frames_f32.shape[1:], jnp.float32), frames_f32], axis=0)
    conv_sum = tap_set[0] * padded[2:] + tap_set[1] * padded[1:-1] + tap_set[2] * padded[:-2]
    mixed_rows = (frames_f32 + conv_sum).astype(jnp.bfloat16)
    head_size = D // HEADS
    group_cols = D // N_SPACE
    group_ff = FF // N_SPACE

    def one_frame(frame_rows):
        frame_f32 = frame_rows.astype(jnp.float32)
        attn_in = modulated(frame_f32, mod_table[0], mod_table[1])
        projected = jnp.dot(attn_in, query_w.reshape(D, 3 * D), preferred_element_type=jnp.float32).astype(jnp.bfloat16)
        projected = projected.reshape(HW, 3, HEADS, head_size).astype(jnp.float32)
        scores = jnp.einsum('qhe,khe->hqk', projected[:, 0], projected[:, 1]) * (1.0 / math.sqrt(head_size))
        probs = jax.nn.softmax(scores, axis=-1).astype(jnp.bfloat16)
        heads_out = jnp.einsum('hqk,khe->qhe', probs.astype(jnp.float32), projected[:, 2]).astype(jnp.bfloat16)
        heads_out = heads_out.reshape(HW, N_SPACE, group_cols).astype(jnp.float32)
        grouped = jnp.einsum('qgk,gkd->gqd', heads_out, out_w.reshape(N_SPACE, group_cols, D).astype(jnp.float32))
        attn_sum = lax.optimization_barrier(jnp.sum(grouped.astype(jnp.bfloat16).astype(jnp.float32), axis=0))
        hidden_state = frame_f32 + mod_table[2] * attn_sum
        mlp_in = modulated(hidden_state, mod_table[3], mod_table[4])
        activated = jax.nn.gelu(jnp.dot(mlp_in, up_w, preferred_element_type=jnp.float32), approximate=True).astype(jnp.bfloat16)
        activated = activated.reshape(HW, N_SPACE, group_ff).astype(jnp.float32)
        grouped_mlp = jnp.einsum('qgk,gkd->gqd', activated, down_w.reshape(N_SPACE, group_ff, D).astype(jnp.float32))
        mlp_sum = lax.optimization_barrier(jnp.sum(grouped_mlp.astype(jnp.bfloat16).astype(jnp.float32), axis=0))
        return (hidden_state + mod_table[5] * mlp_sum).astype(jnp.bfloat16)
    return lax.map(one_frame, mixed_rows)

def reference(video, conv_taps, modulation, w_qkv, w_out, w_up, w_down):
    layer_out = lax.map(one_layer, (video, conv_taps, modulation, w_qkv, w_out, w_up, w_down))
    return jnp.roll(layer_out, 1, axis=0)
```

```python
import functools
import math

import jax
import jax.numpy as jnp
from jax import lax
from jax.experimental import pallas as pl
from jax.experimental.pallas import tpu as pltpu
from jax.sharding import PartitionSpec as P

D = 1152
HEADS = 16
MESH = pl.DeviceIdType.MESH


def normalize(values_in):
    centre = jnp.mean(values_in, axis=-1, keepdims=True)
    variance = jnp.mean(jnp.square(values_in - centre), axis=-1, keepdims=True)
    return (values_in - centre) * lax.rsqrt(variance + 1e-06)


def modulated(values_in, shift_row, scale_row):
    return (normalize(values_in) * (1.0 + scale_row) + shift_row).astype(jnp.bfloat16)


def dot(a, b, dims=((1,), (0,))):
    return lax.dot_general(a, b, (dims, ((), ())), preferred_element_type=jnp.float32)


def chunks(total, size):
    size = size if total % size == 0 else total
    return [(start, size) for start in range(0, total, size)]


def layer(
    sizes, video, taps, mod, qkv_hbm, out_hbm, up_hbm, down_hbm, result,
    frames, halo, mixed, part, part_in, hidden, heads, active, term, term_in, final,
    qkv_w, out_w, up_w, down_w,
    local_sem, halo_send, halo_recv, mix_send, mix_recv, part_send, part_recv,
    term_send, term_recv, end_send, end_recv,
):
    n_section, n_tm, n_space = sizes
    n_frames, tokens, width = frames.shape
    row = n_space * tokens
    section = lax.axis_index("section")
    tm = lax.axis_index("tm")
    me = lax.axis_index("space")
    after = lax.rem(section + 1, n_section)
    before = lax.rem(section + n_section - 1, n_section)
    peers = [lax.rem(me + j, n_space) for j in range(1, n_space)]
    order = list(range(n_frames - 1, -1, -1))

    video_copy = pltpu.make_async_copy(video.at[0], frames, local_sem.at[0])
    video_copy.start()
    weights = [
        pltpu.make_async_copy(source.at[0], target, local_sem.at[1 + i])
        for i, (source, target) in enumerate(
            ((qkv_hbm, qkv_w), (out_hbm, out_w), (up_hbm, up_w), (down_hbm, down_w))
        )
    ]
    for copy in weights:
        copy.start()

    barrier = pltpu.get_barrier_semaphore()
    for peer in peers:
        pl.semaphore_signal(barrier, inc=1, device_id={"space": peer}, device_id_type=MESH)
    for neighbour in (before, after):
        pl.semaphore_signal(barrier, inc=1, device_id={"section": neighbour}, device_id_type=MESH)

    @pl.when(tm > 0)
    def _():
        pl.semaphore_signal(barrier, inc=1, device_id={"tm": tm - 1}, device_id_type=MESH)

    @pl.when(tm < n_tm - 1)
    def _():
        pl.semaphore_signal(barrier, inc=1, device_id={"tm": tm + 1}, device_id_type=MESH)

    along_tm = lax.div(tm + n_tm - 1, n_tm) + 1 - lax.div(tm + 1, n_tm)
    pl.semaphore_wait(barrier, n_space + 1 + along_tm)

    halo_copies = [
        pltpu.make_async_remote_copy(
            src_ref=video.at[0, n_frames - 2 + i],
            dst_ref=halo.at[i],
            send_sem=halo_send.at[i],
            recv_sem=halo_recv.at[i],
            device_id={"tm": lax.rem(tm + 1, n_tm)},
            device_id_type=MESH,
        )
        for i in range(2)
    ]

    @pl.when(tm < n_tm - 1)
    def _():
        halo_copies[1].start()
        halo_copies[0].start()

    @pl.when(tm == 0)
    def _():
        halo[...] = jnp.zeros_like(halo)

    video_copy.wait()

    mix_copies = {}
    arrived = set()
    for f in order:
        terms = []
        for step in range(3):
            at = f - step
            if at >= 0:
                terms.append(frames[at])
            else:
                slot = at + 2
                if slot not in arrived:
                    arrived.add(slot)

                    @pl.when(tm > 0)
                    def _():
                        halo_copies[slot].wait_recv()

                terms.append(halo[slot])
        current, previous, second = (t.astype(jnp.float32) for t in terms)
        mixed[f, me] = (
            current + taps[0] * current + taps[1] * previous + taps[2] * second
        ).astype(jnp.bfloat16)
        for j, peer in enumerate(peers):
            mix_copies[f, j] = pltpu.make_async_remote_copy(
                src_ref=mixed.at[f, me],
                dst_ref=mixed.at[f, me],
                send_sem=mix_send.at[f, j],
                recv_sem=mix_recv.at[f, j],
                device_id={"space": peer},
                device_id_type=MESH,
            )
            mix_copies[f, j].start()

    part_copies = {}
    head_size = D // HEADS
    scale = 1.0 / math.sqrt(head_size)
    for position, f in enumerate(order):
        for j in range(len(peers)):
            mix_copies[f, j].wait_recv()
        rows = mixed[f].reshape(row, width).astype(jnp.float32)
        attn_in = modulated(rows, mod[0], mod[1])
        if position == 0:
            weights[0].wait()
        queries, keys, values = (dot(qkv_w[c], attn_in, ((1,), (1,))) for c in range(3))
        for h in range(queries.shape[0] // head_size):
            span = slice(h * head_size, (h + 1) * head_size)
            key_rows = keys[span].T.astype(jnp.bfloat16)
            scores = dot(key_rows, queries[span].astype(jnp.bfloat16)) * scale
            shifted = jnp.exp(scores - jnp.max(scores, axis=0, keepdims=True))
            probs = shifted / jnp.sum(shifted, axis=0, keepdims=True)
            heads[span] = dot(values[span].astype(jnp.bfloat16), probs.astype(jnp.bfloat16))
        heads_out = heads[...].T.astype(jnp.bfloat16)
        if position == 0:
            weights[1].wait()
        for start, size in chunks(width, 384):
            part[f, :, start : start + size] = dot(
                heads_out, out_w[:, start : start + size]
            ).astype(jnp.bfloat16)
        for j, peer in enumerate(peers):
            part_copies[f, j] = pltpu.make_async_remote_copy(
                src_ref=part.at[f],
                dst_ref=part_in.at[f, j],
                send_sem=part_send.at[f, j],
                recv_sem=part_recv.at[f, j],
                device_id={"space": peer},
                device_id_type=MESH,
            )
            part_copies[f, j].start()

    term_copies = {}
    for position, f in enumerate(order):
        for j in range(len(peers)):
            part_copies[f, j].wait_recv()
        attn_sum = part[f].astype(jnp.float32)
        for j in range(len(peers)):
            attn_sum = attn_sum + part_in[f, j].astype(jnp.float32)
        state = mixed[f].reshape(row, width).astype(jnp.float32) + mod[2] * attn_sum
        hidden[f] = state.reshape(n_space, tokens, width)
        mlp_in = modulated(state, mod[3], mod[4])
        if position == 0:
            weights[2].wait()
        for start, size in chunks(up_w.shape[1], 768):
            active[:, start : start + size] = jax.nn.gelu(
                dot(mlp_in, up_w[:, start : start + size]), approximate=True
            ).astype(jnp.bfloat16)
        if position == 0:
            weights[3].wait()
        for start, size in chunks(width, 384):
            term[f, :, :, start : start + size] = (
                dot(active[...], down_w[:, start : start + size])
                .astype(jnp.bfloat16)
                .reshape(n_space, tokens, size)
            )
        for j, peer in enumerate(peers):
            term_copies[f, j] = pltpu.make_async_remote_copy(
                src_ref=term.at[f, peer],
                dst_ref=term_in.at[f, j],
                send_sem=term_send.at[f, j],
                recv_sem=term_recv.at[f, j],
                device_id={"space": peer},
                device_id_type=MESH,
            )
            term_copies[f, j].start()

    end_copies = []
    for f in order:
        for j in range(len(peers)):
            term_copies[f, j].wait_recv()
        mlp_sum = term[f, me].astype(jnp.float32)
        for j in range(len(peers)):
            mlp_sum = mlp_sum + term_in[f, j].astype(jnp.float32)
        final[f] = (hidden[f, me] + mod[5] * mlp_sum).astype(jnp.bfloat16)
        copy = pltpu.make_async_remote_copy(
            src_ref=final.at[f],
            dst_ref=result.at[0, f],
            send_sem=end_send.at[f],
            recv_sem=end_recv.at[f],
            device_id={"section": after},
            device_id_type=MESH,
        )
        copy.start()
        end_copies.append(copy)

    @pl.when(tm < n_tm - 1)
    def _():
        for copy in halo_copies:
            copy.wait_send()

    for group in (mix_copies, part_copies, term_copies):
        for copy in group.values():
            copy.wait_send()
    for copy in end_copies:
        copy.wait()


def body(sizes, video, conv_taps, modulation, w_qkv, w_out, w_up, w_down):
    n_space = sizes[2]
    _, n_frames, tokens, width = video.shape
    row = n_space * tokens
    columns = w_qkv.shape[3]
    units = w_up.shape[2]
    bf16, f32 = jnp.bfloat16, jnp.float32
    others = max(n_space - 1, 1)
    sem = pltpu.SemaphoreType.DMA
    anywhere = pl.BlockSpec(memory_space=pl.ANY)
    vmem = pl.BlockSpec(memory_space=pltpu.VMEM)
    total = n_frames * row
    return pl.pallas_call(
        functools.partial(layer, sizes),
        out_shape=jax.ShapeDtypeStruct(video.shape, bf16),
        in_specs=[anywhere, vmem, vmem, anywhere, anywhere, anywhere, anywhere],
        out_specs=anywhere,
        scratch_shapes=[
            pltpu.VMEM((n_frames, tokens, width), bf16),
            pltpu.VMEM((2, tokens, width), bf16),
            pltpu.VMEM((n_frames, n_space, tokens, width), bf16),
            pltpu.VMEM((n_frames, row, width), bf16),
            pltpu.VMEM((n_frames, others, row, width), bf16),
            pltpu.VMEM((n_frames, n_space, tokens, width), f32),
            pltpu.VMEM((columns, row), f32),
            pltpu.VMEM((row, units), bf16),
            pltpu.VMEM((n_frames, n_space, tokens, width), bf16),
            pltpu.VMEM((n_frames, others, tokens, width), bf16),
            pltpu.VMEM((n_frames, tokens, width), bf16),
            pltpu.VMEM((3, columns, width), bf16),
            pltpu.VMEM((columns, width), bf16),
            pltpu.VMEM((width, units), bf16),
            pltpu.VMEM((units, width), bf16),
            sem((5,)),
            sem((2,)),
            sem((2,)),
            sem((n_frames, others)),
            sem((n_frames, others)),
            sem((n_frames, others)),
            sem((n_frames, others)),
            sem((n_frames, others)),
            sem((n_frames, others)),
            sem((n_frames,)),
            sem((n_frames,)),
        ],
        compiler_params=pltpu.CompilerParams(
            collective_id=0, has_side_effects=True, vmem_limit_bytes=56 * 1024 * 1024
        ),
        cost_estimate=pl.CostEstimate(
            flops=2 * total * width * (4 * columns + 2 * units),
            bytes_accessed=2 * width * (4 * columns + 2 * units),
            transcendentals=total * units,
        ),
    )(
        video,
        jnp.transpose(conv_taps, (1, 0, 2)),
        jnp.transpose(modulation, (1, 0, 2)),
        jnp.transpose(w_qkv, (0, 2, 3, 1)),
        w_out,
        w_up,
        w_down,
    )


def solution(mesh):
    sizes = (mesh.shape["section"], mesh.shape["tm"], mesh.shape["space"])
    placed = (
        P("section", "tm", "space", None),
        P("section", None, None),
        P("section", None, None),
        P("section", None, None, "space"),
        P("section", "space", None),
        P("section", None, "space"),
        P("section", "space", None),
    )
    return jax.shard_map(
        functools.partial(body, sizes),
        mesh=mesh,
        in_specs=placed,
        out_specs=P("section", "tm", "space", None),
        check_vma=False,
    )
```

```python
import functools
import math

import jax
import jax.numpy as jnp
from jax import lax
from jax.experimental import pallas as pl
from jax.experimental.pallas import tpu as pltpu
from jax.sharding import PartitionSpec as P

D = 1152
HEADS = 16
MESH = pl.DeviceIdType.MESH
PIECES = 4
SPAN = 384


def normalize(values_in):
    centre = jnp.mean(values_in, axis=-1, keepdims=True)
    variance = jnp.mean(jnp.square(values_in - centre), axis=-1, keepdims=True)
    return (values_in - centre) * lax.rsqrt(variance + 1e-06)


def modulated(values_in, shift_row, scale_row):
    return (normalize(values_in) * (1.0 + scale_row) + shift_row).astype(jnp.bfloat16)


def dot(a, b, dims=((1,), (0,))):
    return lax.dot_general(a, b, (dims, ((), ())), preferred_element_type=jnp.float32)


def chunks(total, size):
    size = size if total % size == 0 else total
    return [(start, size) for start in range(0, total, size)]


def row_pieces(tokens):
    count = PIECES if tokens % (16 * PIECES) == 0 else 1
    return [(i * (tokens // count), tokens // count) for i in range(count)]


def layer(
    sizes, video, taps, mod, qkv_hbm, out_hbm, up_hbm, down_hbm, result,
    frames, halo, mixed, part, part_in, hidden, heads, active, term, term_in, final,
    qkv_w, out_w, up_w, down_w,
    local_sem, halo_send, halo_recv, mix_send, mix_recv, part_send, part_recv,
    term_send, term_recv, end_send, end_recv,
):
    n_section, n_tm, n_space = sizes
    n_frames, tokens, width = frames.shape
    row = n_space * tokens
    section = lax.axis_index("section")
    tm = lax.axis_index("tm")
    me = lax.axis_index("space")
    after = lax.rem(section + 1, n_section)
    before = lax.rem(section + n_section - 1, n_section)
    peers = [lax.rem(me + j, n_space) for j in range(1, n_space)]
    order = list(range(n_frames - 1, -1, -1))

    video_copy = pltpu.make_async_copy(video.at[0], frames, local_sem.at[0])
    video_copy.start()
    weights = [
        pltpu.make_async_copy(source.at[0], target, local_sem.at[1 + i])
        for i, (source, target) in enumerate(
            ((qkv_hbm, qkv_w), (out_hbm, out_w), (up_hbm, up_w), (down_hbm, down_w))
        )
    ]
    weights[0].start()

    barrier = pltpu.get_barrier_semaphore()
    for peer in peers:
        pl.semaphore_signal(barrier, inc=1, device_id={"space": peer}, device_id_type=MESH)
    for neighbour in (before, after):
        pl.semaphore_signal(barrier, inc=1, device_id={"section": neighbour}, device_id_type=MESH)

    @pl.when(tm > 0)
    def _():
        pl.semaphore_signal(barrier, inc=1, device_id={"tm": tm - 1}, device_id_type=MESH)

    @pl.when(tm < n_tm - 1)
    def _():
        pl.semaphore_signal(barrier, inc=1, device_id={"tm": tm + 1}, device_id_type=MESH)

    along_tm = lax.div(tm + n_tm - 1, n_tm) + 1 - lax.div(tm + 1, n_tm)
    pl.semaphore_wait(barrier, n_space + 1 + along_tm)

    video_copy.wait()
    pieces = row_pieces(tokens)
    halo_copies = {
        (i, p): pltpu.make_async_remote_copy(
            src_ref=frames.at[n_frames - 2 + i, pl.ds(start, size)],
            dst_ref=halo.at[i, pl.ds(start, size)],
            send_sem=halo_send.at[i, p],
            recv_sem=halo_recv.at[i, p],
            device_id={"tm": lax.rem(tm + 1, n_tm)},
            device_id_type=MESH,
        )
        for i in (1, 0)
        for p, (start, size) in enumerate(pieces)
    }

    @pl.when(tm < n_tm - 1)
    def _():
        for copy in halo_copies.values():
            copy.start()

    @pl.when(tm == 0)
    def _():
        halo[...] = jnp.zeros_like(halo)

    for copy in weights[1:]:
        copy.start()

    mix_copies = {}
    arrived = set()
    for f in order:
        for p, (start, size) in enumerate(pieces):
            rows = slice(start, start + size)
            terms = []
            for step in range(3):
                at = f - step
                if at >= 0:
                    terms.append(frames[at, rows])
                else:
                    slot = at + 2
                    if (slot, p) not in arrived:
                        arrived.add((slot, p))

                        @pl.when(tm > 0)
                        def _():
                            halo_copies[slot, p].wait_recv()

                    terms.append(halo[slot, rows])
            current, previous, second = (t.astype(jnp.float32) for t in terms)
            mixed[f, me, rows] = (
                current + taps[0] * current + taps[1] * previous + taps[2] * second
            ).astype(jnp.bfloat16)
            for j, peer in enumerate(peers):
                mix_copies[f, j, p] = pltpu.make_async_remote_copy(
                    src_ref=mixed.at[f, me, pl.ds(start, size)],
                    dst_ref=mixed.at[f, me, pl.ds(start, size)],
                    send_sem=mix_send.at[f, j, p],
                    recv_sem=mix_recv.at[f, j, p],
                    device_id={"space": peer},
                    device_id_type=MESH,
                )
                mix_copies[f, j, p].start()

    part_copies = {}
    spans = chunks(width, SPAN)
    head_size = D // HEADS
    scale = 1.0 / math.sqrt(head_size)
    for position, f in enumerate(order):
        for j in range(len(peers)):
            for p in range(len(pieces)):
                mix_copies[f, j, p].wait_recv()
        rows = mixed[f].reshape(row, width).astype(jnp.float32)
        attn_in = modulated(rows, mod[0], mod[1])
        if position == 0:
            weights[0].wait()
        queries, keys, values = (dot(qkv_w[c], attn_in, ((1,), (1,))) for c in range(3))
        for h in range(queries.shape[0] // head_size):
            span = slice(h * head_size, (h + 1) * head_size)
            key_rows = keys[span].T.astype(jnp.bfloat16)
            scores = dot(key_rows, queries[span].astype(jnp.bfloat16)) * scale
            shifted = jnp.exp(scores - jnp.max(scores, axis=0, keepdims=True))
            probs = shifted / jnp.sum(shifted, axis=0, keepdims=True)
            heads[span] = dot(values[span].astype(jnp.bfloat16), probs.astype(jnp.bfloat16))
        heads_out = heads[...].T.astype(jnp.bfloat16)
        if position == 0:
            weights[1].wait()
        for p, (start, size) in enumerate(spans):
            part[f, :, start : start + size] = dot(
                heads_out, out_w[:, start : start + size]
            ).astype(jnp.bfloat16)
            for j, peer in enumerate(peers):
                part_copies[f, j, p] = pltpu.make_async_remote_copy(
                    src_ref=part.at[f, :, pl.ds(start, size)],
                    dst_ref=part_in.at[f, j, :, pl.ds(start, size)],
                    send_sem=part_send.at[f, j, p],
                    recv_sem=part_recv.at[f, j, p],
                    device_id={"space": peer},
                    device_id_type=MESH,
                )
                part_copies[f, j, p].start()

    term_copies = {}
    for position, f in enumerate(order):
        for j in range(len(peers)):
            for p in range(len(spans)):
                part_copies[f, j, p].wait_recv()
        attn_sum = part[f].astype(jnp.float32)
        for j in range(len(peers)):
            attn_sum = attn_sum + part_in[f, j].astype(jnp.float32)
        state = mixed[f].reshape(row, width).astype(jnp.float32) + mod[2] * attn_sum
        hidden[f] = state.reshape(n_space, tokens, width)
        mlp_in = modulated(state, mod[3], mod[4])
        if position == 0:
            weights[2].wait()
        for start, size in chunks(up_w.shape[1], 768):
            active[:, start : start + size] = jax.nn.gelu(
                dot(mlp_in, up_w[:, start : start + size]), approximate=True
            ).astype(jnp.bfloat16)
        if position == 0:
            weights[3].wait()
        for p, (start, size) in enumerate(spans):
            term[f, :, :, start : start + size] = (
                dot(active[...], down_w[:, start : start + size])
                .astype(jnp.bfloat16)
                .reshape(n_space, tokens, size)
            )
            for j, peer in enumerate(peers):
                term_copies[f, j, p] = pltpu.make_async_remote_copy(
                    src_ref=term.at[f, peer, :, pl.ds(start, size)],
                    dst_ref=term_in.at[f, j, :, pl.ds(start, size)],
                    send_sem=term_send.at[f, j, p],
                    recv_sem=term_recv.at[f, j, p],
                    device_id={"space": peer},
                    device_id_type=MESH,
                )
                term_copies[f, j, p].start()

    end_copies = []
    for f in order:
        for p, (start, size) in enumerate(spans):
            span = slice(start, start + size)
            for j in range(len(peers)):
                term_copies[f, j, p].wait_recv()
            mlp_sum = term[f, me, :, span].astype(jnp.float32)
            for j in range(len(peers)):
                mlp_sum = mlp_sum + term_in[f, j, :, span].astype(jnp.float32)
            final[f, :, span] = (hidden[f, me, :, span] + mod[5, :, span] * mlp_sum).astype(
                jnp.bfloat16
            )
            copy = pltpu.make_async_remote_copy(
                src_ref=final.at[f, :, pl.ds(start, size)],
                dst_ref=result.at[0, f, :, pl.ds(start, size)],
                send_sem=end_send.at[f, p],
                recv_sem=end_recv.at[f, p],
                device_id={"section": after},
                device_id_type=MESH,
            )
            copy.start()
            end_copies.append(copy)

    @pl.when(tm < n_tm - 1)
    def _():
        for copy in halo_copies.values():
            copy.wait_send()

    for group in (mix_copies, part_copies, term_copies):
        for copy in group.values():
            copy.wait_send()
    for copy in end_copies:
        copy.wait()


def body(sizes, video, conv_taps, modulation, w_qkv, w_out, w_up, w_down):
    n_space = sizes[2]
    _, n_frames, tokens, width = video.shape
    row = n_space * tokens
    columns = w_qkv.shape[3]
    units = w_up.shape[2]
    bf16, f32 = jnp.bfloat16, jnp.float32
    others = max(n_space - 1, 1)
    sem = pltpu.SemaphoreType.DMA
    anywhere = pl.BlockSpec(memory_space=pl.ANY)
    vmem = pl.BlockSpec(memory_space=pltpu.VMEM)
    total = n_frames * row
    n_pieces, n_spans = len(row_pieces(tokens)), len(chunks(width, SPAN))
    return pl.pallas_call(
        functools.partial(layer, sizes),
        out_shape=jax.ShapeDtypeStruct(video.shape, bf16),
        in_specs=[anywhere, vmem, vmem, anywhere, anywhere, anywhere, anywhere],
        out_specs=anywhere,
        scratch_shapes=[
            pltpu.VMEM((n_frames, tokens, width), bf16),
            pltpu.VMEM((2, tokens, width), bf16),
            pltpu.VMEM((n_frames, n_space, tokens, width), bf16),
            pltpu.VMEM((n_frames, row, width), bf16),
            pltpu.VMEM((n_frames, others, row, width), bf16),
            pltpu.VMEM((n_frames, n_space, tokens, width), f32),
            pltpu.VMEM((columns, row), f32),
            pltpu.VMEM((row, units), bf16),
            pltpu.VMEM((n_frames, n_space, tokens, width), bf16),
            pltpu.VMEM((n_frames, others, tokens, width), bf16),
            pltpu.VMEM((n_frames, tokens, width), bf16),
            pltpu.VMEM((3, columns, width), bf16),
            pltpu.VMEM((columns, width), bf16),
            pltpu.VMEM((width, units), bf16),
            pltpu.VMEM((units, width), bf16),
            sem((5,)),
            sem((2, n_pieces)),
            sem((2, n_pieces)),
            sem((n_frames, others, n_pieces)),
            sem((n_frames, others, n_pieces)),
            sem((n_frames, others, n_spans)),
            sem((n_frames, others, n_spans)),
            sem((n_frames, others, n_spans)),
            sem((n_frames, others, n_spans)),
            sem((n_frames, n_spans)),
            sem((n_frames, n_spans)),
        ],
        compiler_params=pltpu.CompilerParams(
            collective_id=0, has_side_effects=True, vmem_limit_bytes=56 * 1024 * 1024
        ),
        cost_estimate=pl.CostEstimate(
            flops=2 * total * width * (4 * columns + 2 * units),
            bytes_accessed=2 * width * (4 * columns + 2 * units),
            transcendentals=total * units,
        ),
    )(
        video,
        jnp.transpose(conv_taps, (1, 0, 2)),
        jnp.transpose(modulation, (1, 0, 2)),
        jnp.transpose(w_qkv, (0, 2, 3, 1)),
        w_out,
        w_up,
        w_down,
    )


def solution(mesh):
    sizes = (mesh.shape["section"], mesh.shape["tm"], mesh.shape["space"])
    placed = (
        P("section", "tm", "space", None),
        P("section", None, None),
        P("section", None, None),
        P("section", None, None, "space"),
        P("section", "space", None),
        P("section", None, "space"),
        P("section", "space", None),
    )
    return jax.shard_map(
        functools.partial(body, sizes),
        mesh=mesh,
        in_specs=placed,
        out_specs=P("section", "tm", "space", None),
        check_vma=False,
    )
```
